512 devices in a mesh: ctx: 64 (over z_hi, x, y), tp: 8 (over z_lo, core).
Axes of the slice: x: 4, y: 4, z: 16 (z_hi: 4, z_lo: 4; z = z_hi * 4 + z_lo), core: 2. Of those that a mesh axis runs over, the one named last changes fastest.
Arguments:
- queries: bfloat16 [8192, 32, 128], P('ctx', 'tp'), may hold values from -14 to 14
- keys: bfloat16 [8192, 4, 128], P('ctx'), may hold values from -14 to 14
- values: bfloat16 [8192, 4, 128], P('ctx'), may hold values from -6 to 6
- segment_ids: int32 [8192], P('ctx'), may hold values from 0 to 1, never falling along the last dimension, each value on 1 to 6144 neighbouring positions
- out_weight: bfloat16 [4096, 8192], P('tp', 'ctx'), may hold values from -0.375 to 0.375
Outputs:
- projected: bfloat16 [8192, 8192], P('ctx', 'tp')
The draws below stay inside these ranges and needn't reach their ends.
Inputs may be any that keep to these rules, and one draw needn't show every extreme that they name: `segment_ids`: document ids never fall along the window; the longest document holds at most 6144 tokens.
All inputs are finite; a program needn't handle non-finite values.
Results may differ from the reference program's by a relative error of at most 0.017.
Values may be sent and summed in bfloat16 or wider, within the bound.
A program may use at most 128 MiB of HBM per device.

```python
import math
import jax
import jax.numpy as jnp
import numpy as np
from jax import lax

D = 8192
HQ = 32
KVH = 4
HD = 128
QB = 128
TOKENS = 8192
N_TP = 8


def draw_queries(key, part):
    key = jax.random.fold_in(key, 1)
    own = jnp.clip(2.0 * jax.random.normal(key, (TOKENS, HQ, HD), jnp.float32), -14.0, 14.0)
    return own.astype(jnp.bfloat16)


def draw_keys(key, part):
    key = jax.random.fold_in(key, 2)
    own = jnp.clip(jax.random.normal(key, (TOKENS, KVH, HD), jnp.float32), -6.0, 6.0)
    return own.astype(jnp.bfloat16)


def levels(stream_key, extent, shards, low, largest):
    gain = 1.0
    for axis_at, parts in shards:
        draws = jax.random.uniform(jax.random.fold_in(jax.random.fold_in(stream_key, 6), axis_at), (parts,), jnp.float32, low / len(shards), largest / len(shards))
        gain = gain * jnp.repeat(jnp.exp(draws), extent[axis_at] // parts).reshape((-1,) + (1,) * (len(extent) - 1 - axis_at))
    return gain


def split_up(count, total, limit, slope):
    loads = [(1 << 20) // math.isqrt(grade ** slope) + 1 for grade in range(2, count + 1)]
    surplus, given = total - limit - (count - 1), [1] * (count - 1)
    while surplus > 0:
        free = [i for i in range(count - 1) if given[i] < limit]
        whole, remaining = sum([loads[i] for i in free]), surplus
        for i in free:
            extra = min(limit - given[i], max(1, remaining * loads[i] // whole), surplus)
            given[i] = given[i] + extra
            surplus = surplus - extra
    return np.array([limit] + given)


def ragged(own_key, count, total, bound, lean):
    if count == 2:
        one = jax.random.randint(own_key, (), max(1, total - bound), min(bound, total - 1) + 1)
        return jnp.stack([one, total - one])
    lengths = jnp.asarray(split_up(count, total, bound, lean), jnp.int32)
    pairs = (count - 1) // 2
    source_of, receiver = lengths[1:1 + 2 * pairs:2], lengths[2:2 + 2 * pairs:2]
    margin = jnp.minimum(source_of - 1, bound - receiver)
    moved = jax.random.randint(jax.random.fold_in(own_key, 1), (pairs,), 0, 1 << 20) % (margin + 1)
    lengths = lengths.at[1:1 + 2 * pairs:2].set(source_of - moved).at[2:2 + 2 * pairs:2].set(receiver + moved)
    return lengths[jax.random.permutation(jax.random.fold_in(own_key, 2), count)]


def bell_draw(stream_key, dims, spread, reach, cuts=(), dtype=jnp.bfloat16):
    values = spread * jax.random.normal(stream_key, dims, jnp.float32)
    if cuts:
        values = values * levels(stream_key, dims, cuts, -0.22, 0.18)
    return jnp.clip(values, -reach, reach).astype(dtype)


def setup_inputs(seed: int = 0) -> dict:
    seeds = jax.random.split(jax.random.key(seed), 6)
    queries = draw_queries(jax.random.fold_in(seeds[5], 71), 0)
    keys = draw_keys(jax.random.fold_in(seeds[5], 71), 0)
    values = bell_draw(seeds[2], (TOKENS, KVH, HD), 1.0, 6.0, ((0, 64),))
    segment_ids = jnp.searchsorted(jnp.cumsum(ragged(seeds[3], 2, TOKENS, 3 * TOKENS // 4, 0)), jnp.arange(TOKENS), side="right").astype(jnp.int32)
    out_weight = bell_draw(seeds[4], (HQ * HD, D), (HQ * HD // 16) ** -0.5, 0.375, ((0, 8), (1, 64)))
    return {"queries": queries, "keys": keys, "values": values, "segment_ids": segment_ids, "out_weight": out_weight}


def hadamard_table(order_size):
    position = jnp.arange(order_size)
    parity = jnp.zeros((order_size, order_size), jnp.int32)
    for level in range(order_size.bit_length() - 1):
        step_bit = 2 ** level
        parity = parity + position[:, None] // step_bit % 2 * (position[None, :] // step_bit % 2)
    return jnp.where(parity % 2 == 0, 1.0, -1.0).astype(jnp.float32) / math.sqrt(order_size)

def rotate_blocks(partial_value):
    row_count, col_count = partial_value.shape
    rotation = hadamard_table(QB)
    result = jnp.einsum('rbq,qp->rbp', partial_value.reshape(row_count, col_count // QB, QB), rotation, precision=lax.Precision.HIGHEST)
    return result.reshape(row_count, col_count)

def attend(queries, keys, values, segment_ids):
    group_size = HQ // KVH
    score_scale = HD ** (-0.5)
    block_rows = min(512, TOKENS)
    positions = jnp.arange(TOKENS).astype(jnp.int32)

    def per_head(kv_head):
        head_queries = lax.dynamic_slice_in_dim(queries, kv_head * group_size, group_size, 1).astype(jnp.float32)
        head_keys = lax.dynamic_index_in_dim(keys, kv_head, 1, keepdims=False).astype(jnp.float32)
        head_values = lax.dynamic_index_in_dim(values, kv_head, 1, keepdims=False).astype(jnp.float32)

        def per_block(block_index):
            first_row = (block_index * block_rows).astype(jnp.int32)
            block_queries = lax.dynamic_slice_in_dim(head_queries, first_row, block_rows, 0)
            query_pos = first_row + jnp.arange(block_rows).astype(jnp.int32)
            query_seg = lax.dynamic_slice_in_dim(segment_ids, first_row, block_rows, 0)
            scores = jnp.einsum('tgd,kd->tgk', block_queries, head_keys, precision=lax.Precision.HIGHEST) * score_scale
            allowed = (query_seg[:, None] == segment_ids[None, :]) & (positions[None, :] <= query_pos[:, None])
            allowed = allowed[:, None, :]
            scores = jnp.where(allowed, scores, -1e+30)
            top_score = lax.optimization_barrier(jnp.max(scores, axis=-1, keepdims=True))
            weights = jnp.where(allowed, jnp.exp(scores - top_score), 0.0)
            output = jnp.einsum('tgk,kd->tgd', weights, head_values, precision=lax.Precision.HIGHEST)
            return output / lax.optimization_barrier(jnp.sum(weights, axis=-1))[..., None]
        blocks = lax.map(per_block, jnp.arange(TOKENS // block_rows).astype(jnp.int32))
        return blocks.reshape(TOKENS, group_size, HD)
    heads_out = lax.map(per_head, jnp.arange(KVH).astype(jnp.int32))
    heads_out = jnp.transpose(heads_out, (1, 0, 2, 3)).reshape(TOKENS, HQ * HD)
    return heads_out.astype(jnp.bfloat16)

def reference(queries, keys, values, segment_ids, out_weight):
    attended = attend(queries, keys, values, segment_ids)
    group_rows = HQ * HD // N_TP
    summed = jnp.zeros((TOKENS, D), jnp.float32)
    for group_index in range(N_TP):
        lower = group_index * group_rows
        partial_value = jnp.dot(attended[:, lower:lower + group_rows], out_weight[lower:lower + group_rows], preferred_element_type=jnp.float32)
        rotated = lax.optimization_barrier(rotate_blocks(partial_value).astype(jnp.bfloat16))
        summed = summed + rotated.astype(jnp.float32)
    return summed.astype(jnp.bfloat16)
```

```python
import functools
import math

import jax
import jax.numpy as jnp
from jax import lax
from jax.experimental import pallas as pl
from jax.experimental.pallas import tpu as pltpu
from jax.sharding import PartitionSpec as P

HQ = 32
KVH = 4
HD = 128
ROWS = 128
SEG = 16
BLK = ROWS + SEG
NEG = -1e30
MESH = pl.DeviceIdType.MESH
BF16, F32 = jnp.bfloat16, jnp.float32


def mod4(value):
    return lax.rem(value + 8, 4)


def hadamard_signs():
    both = lax.broadcasted_iota(jnp.int32, (HD, HD), 0) & lax.broadcasted_iota(jnp.int32, (HD, HD), 1)
    both = both ^ (both >> 4)
    both = both ^ (both >> 2)
    both = both ^ (both >> 1)
    return (1 - 2 * (both & 1)).astype(F32).astype(BF16)


def kernel(
    q_ref, mine_ref, seg_ref, w_ref, o_ref,
    kv, wb, asrc, ar, pbuf, rb, osrc, ob, segq, top, den, acc,
    kz_s, kz_r, kp_s, kp_r, ks_s, ks_r, wz_s, wz_r, wx_s, wx_r, ws_s, ws_r, a_s, a_r, p_s, p_r, o_s, o_r,
):
    ctx, tpi = lax.axis_index("ctx"), lax.axis_index("tp")
    h, x, y = lax.div(ctx, 16), lax.rem(lax.div(ctx, 4), 4), lax.rem(ctx, 4)
    z, k = lax.div(tpi, 2), lax.rem(tpi, 2)
    xy = x * 4 + y
    other = 1 - k

    def dev(dh=0, dx=0, dy=0, dz=0, core=None):
        return (
            mod4(h + dh) * 16 + mod4(x + dx) * 4 + mod4(y + dy),
            mod4(z + dz) * 2 + (k if core is None else core),
        )

    def copy(src, dst, send, recv, device):
        return pltpu.make_async_remote_copy(
            src_ref=src, dst_ref=dst, send_sem=send, recv_sem=recv, device_id=device, device_id_type=MESH
        )

    sib = dev(core=other)

    barrier = pltpu.get_barrier_semaphore()

    def greet(device):
        pl.semaphore_signal(barrier, inc=1, device_id=device, device_id_type=MESH)

    greet(sib)
    for i in range(1, 4):
        greet(dev(dh=i))
        greet(dev(dz=i))
        greet(dev(dy=i, core=other))

    def greet_plane(d, _):
        greet(dev(dx=lax.div(d, 4), dy=lax.rem(d, 4)))
        return 0

    lax.fori_loop(1, 16, greet_plane, 0)

    kv[k, h, xy, 0:ROWS, :] = mine_ref[...]
    seg_row = seg_ref[...].astype(F32)
    kv[k, h, xy, ROWS:BLK, :] = jnp.broadcast_to(seg_row, (SEG, HD)).astype(BF16)
    rotated = jnp.dot(w_ref[...], hadamard_signs(), preferred_element_type=F32) * (1.0 / math.sqrt(HD))
    wb[k, h, x] = rotated.astype(BF16)
    seg_col = jnp.broadcast_to(seg_row, (ROWS, HD)).T
    for i in range(4):
        segq[i * ROWS : (i + 1) * ROWS, :] = seg_col
    top[...] = jnp.full_like(top, NEG)
    den[...] = jnp.zeros_like(den)
    acc[...] = jnp.zeros_like(acc)

    pl.semaphore_wait(barrier, 25)

    def kv_z(i, out):
        at = kv.at[k, h if out else mod4(h - i), xy]
        return copy(at, at, kz_s.at[i], kz_r.at[i], dev(dh=i))

    def kv_plane(r, d, out):
        dx, dy = lax.div(d, 4), lax.rem(d, 4)
        place = xy if out else mod4(x - dx) * 4 + mod4(y - dy)
        at = kv.at[k, mod4(h - r), place]
        return copy(at, at, kp_s.at[r, d], kp_r.at[r, d], dev(dx=dx, dy=dy))

    def kv_sib(r, dx, out):
        at = kv.at[k if out else other, mod4(h - r), pl.ds(mod4(x - dx) * 4, 4)]
        return copy(at, at, ks_s.at[r, dx], ks_r.at[r, dx], sib)

    def w_z(i, out):
        at = wb.at[k, h if out else mod4(h - i), x]
        return copy(at, at, wz_s.at[i], wz_r.at[i], dev(dh=i))

    def w_x(r, i, out):
        at = wb.at[k, mod4(h - r), x if out else mod4(x - i)]
        return copy(at, at, wx_s.at[r, i], wx_r.at[r, i], dev(dx=i))

    def w_sib(r, out):
        at = wb.at[k if out else other, mod4(h - r)]
        return copy(at, at, ws_s.at[r], ws_r.at[r], sib)

    def a_y(dy, dk, out):
        core = lax.rem(k + dk, 2)
        dst = ar.at[k, y] if out else ar.at[core, mod4(y - dy)]
        return copy(asrc.at[core], dst, a_s.at[dy, dk], a_r.at[dy, dk], dev(dy=dy, core=core))

    def p_z(i, out):
        return copy(pbuf.at[i], rb.at[z if out else mod4(z - i)], p_s.at[i], p_r.at[i], dev(dz=i))

    def o_y(dy, dk, out):
        core = lax.rem(k + dk, 2)
        dst = ob.at[k, y] if out else ob.at[core, mod4(y - dy)]
        return copy(osrc.at[mod4(y + dy), core], dst, o_s.at[dy, dk], o_r.at[dy, dk], dev(dy=dy, core=core))

    pairs = [(dy, dk) for dy in range(4) for dk in range(2) if dy or dk]

    def plane_out(r):
        def step(d, _):
            kv_plane(r, d, True).start()
            return 0

        lax.fori_loop(1, 16, step, 0)

    def plane_in(r):
        def row(dx, _):
            def one(d, _):
                kv_plane(r, d, False).wait_recv()
                return 0

            lax.fori_loop(jnp.maximum(dx * 4, 1), dx * 4 + 4, one, 0)
            kv_sib(r, dx, True).start()
            return 0

        lax.fori_loop(0, 4, row, 0)

    def attend(hp, row, diagonal):
        keys = kv[0, hp, pl.ds(row * 4, 4), 0:ROWS, :].reshape(4 * ROWS, HD)
        values = kv[1, hp, pl.ds(row * 4, 4), 0:ROWS, :].reshape(4 * ROWS, HD)
        ids = kv[0, hp, pl.ds(row * 4, 4), ROWS:BLK, :].astype(F32)
        ids = jnp.concatenate([ids[j, 0:1, :] for j in range(4)], axis=1)
        scores = lax.dot_general(
            q_ref[...], keys, (((1,), (1,)), ((), ())), preferred_element_type=F32
        )
        own = segq[...]
        allowed = ids == jnp.concatenate([own] * 4, axis=1)
        if diagonal:
            place = lax.broadcasted_iota(jnp.int32, scores.shape, 1)
            token = lax.rem(lax.broadcasted_iota(jnp.int32, scores.shape, 0), ROWS) + y * ROWS
            allowed = allowed & (place <= token)
        scores = jnp.where(allowed, scores, NEG)
        before = top[...]
        now = jnp.maximum(before, jnp.max(scores, axis=1, keepdims=True))
        rate = math.log2(math.e) / math.sqrt(HD)
        keep = jnp.exp2((before - now) * rate)
        weights = jnp.exp2((scores - jnp.concatenate([now] * 4, axis=1)) * rate)
        part = (weights[:, 0:128] + weights[:, 128:256]) + (weights[:, 256:384] + weights[:, 384:512])
        top[...] = now
        den[...] = den[...] * keep + part
        acc[...] = acc[...] * keep + jnp.dot(weights.astype(BF16), values, preferred_element_type=F32)

    for i in (1, 3, 2):
        kv_z(i, True).start()
    plane_out(0)
    for i in (1, 3, 2):
        w_z(i, True).start()
    for i in range(1, 4):
        w_x(0, i, True).start()

    for r in (1, 3, 2):
        kv_z(r, False).wait_recv()
        plane_out(r)

    plane_in(0)
    kv_sib(0, 0, False).wait_recv()
    attend(h, x, True)

    def own_rows(dx, _):
        kv_sib(0, dx, False).wait_recv()

        @pl.when(dx <= x)
        def _():
            attend(h, x - dx, False)

        return 0

    lax.fori_loop(1, 4, own_rows, 0)

    for r in (1, 3, 2):
        plane_in(r)

        def rows(dx, _, r=r):
            kv_sib(r, dx, False).wait_recv()

            @pl.when(r <= h)
            def _():
                attend(h - r, mod4(x - dx), False)

            return 0

        lax.fori_loop(0, 4, rows, 0)
        w_z(r, False).wait_recv()
        for i in range(1, 4):
            w_x(r, i, True).start()

    out = acc[...] / jnp.sum(den[...], axis=1, keepdims=True)
    for head in range(4):
        for half in range(2):
            first = head * ROWS + half * 64
            asrc[half, :, head * HD : (head + 1) * HD] = out[first : first + 64].astype(BF16)
    for dy, dk in pairs:
        a_y(dy, dk, True).start()
    ar[k, y] = asrc[k]

    for r in (0, 1, 3, 2):
        for i in range(1, 4):
            w_x(r, i, False).wait_recv()
        w_sib(r, True).start()
    for r in (0, 1, 3, 2):
        w_sib(r, False).wait_recv()

    for dy, dk in pairs:
        a_y(dy, dk, False).wait_recv()

    def partial_for(dest):
        total = None
        for core in range(2):
            rows = ar[core].reshape(4 * 64, 4 * HD)
            columns = jnp.concatenate([wb[core, dest, j] for j in range(4)], axis=1)
            term = jnp.dot(rows, columns, preferred_element_type=F32)
            total = term if total is None else total + term
        return total

    for i in (2, 1, 3):
        pbuf[i] = partial_for(mod4(z + i)).astype(BF16)
        p_z(i, True).start()
    summed = partial_for(z)
    for i in (1, 3, 2):
        p_z(i, False).wait_recv()
        summed = summed + rb[mod4(z - i)].astype(F32)

    summed = summed.astype(BF16)
    for row in range(4):
        for core in range(2):
            for b in range(2):
                col = (core * 2 + b) * HD
                osrc[row, core, b] = summed[row * 64 : (row + 1) * 64, col : col + HD]
    for dy, dk in pairs:
        o_y(dy, dk, True).start()
    ob[k, y] = osrc[y, k]
    for dy, dk in pairs:
        o_y(dy, dk, False).wait_recv()
    for core in range(2):
        for row in range(4):
            for b in range(2):
                col = (b * 4 + row) * HD
                o_ref[core * 64 : (core + 1) * 64, col : col + HD] = ob[core, row, b]

    for i in range(1, 4):
        kv_z(i, True).wait_send()
        w_z(i, True).wait_send()
        p_z(i, True).wait_send()
    for r in range(4):

        def sent(d, _, r=r):
            kv_plane(r, d, True).wait_send()
            return 0

        lax.fori_loop(1, 16, sent, 0)

        def handed(dx, _, r=r):
            kv_sib(r, dx, True).wait_send()
            return 0

        lax.fori_loop(0, 4, handed, 0)
        for i in range(1, 4):
            w_x(r, i, True).wait_send()
        w_sib(r, True).wait_send()
    for dy, dk in pairs:
        a_y(dy, dk, True).wait_send()
        o_y(dy, dk, True).wait_send()


def body(queries, keys, values, segment_ids, out_weight):
    tpi = lax.axis_index("tp")
    head = tpi // 2
    mine = lax.dynamic_index_in_dim(jnp.where(tpi % 2 == 0, keys, values), head, 1, keepdims=False)
    q_rows = jnp.transpose(queries, (1, 0, 2)).reshape(4 * ROWS, HD)
    dma = pltpu.SemaphoreType.DMA
    return pl.pallas_call(
        kernel,
        out_shape=jax.ShapeDtypeStruct((ROWS, 1024), BF16),
        in_specs=[pl.BlockSpec(memory_space=pltpu.VMEM)] * 4,
        out_specs=pl.BlockSpec(memory_space=pltpu.VMEM),
        scratch_shapes=[
            pltpu.VMEM((2, 4, 16, BLK, HD), BF16),
            pltpu.VMEM((2, 4, 4, 512, HD), BF16),
            pltpu.VMEM((2, 64, 512), BF16),
            pltpu.VMEM((2, 4, 64, 512), BF16),
            pltpu.VMEM((4, 256, 512), BF16),
            pltpu.VMEM((4, 256, 512), BF16),
            pltpu.VMEM((4, 2, 2, 64, HD), BF16),
            pltpu.VMEM((2, 4, 2, 64, HD), BF16),
            pltpu.VMEM((512, HD), F32),
            pltpu.VMEM((512, HD), F32),
            pltpu.VMEM((512, HD), F32),
            pltpu.VMEM((512, HD), F32),
        ]
        + [dma((4,))] * 2
        + [dma((4, 16))] * 2
        + [dma((4, 4))] * 2
        + [dma((4,))] * 2
        + [dma((4, 4))] * 2
        + [dma((4,))] * 2
        + [dma((4, 2))] * 2
        + [dma((4,))] * 2
        + [dma((4, 2))] * 2,
        compiler_params=pltpu.CompilerParams(
            collective_id=0, has_side_effects=True, vmem_limit_bytes=48 << 20
        ),
        name="attention_projection",
    )(q_rows, mine, segment_ids.reshape(1, ROWS), out_weight)


def solution(mesh):
    in_specs = (
        P("ctx", "tp", None),
        P("ctx", None, None),
        P("ctx", None, None),
        P("ctx"),
        P("tp", "ctx"),
    )
    return jax.shard_map(body, mesh=mesh, in_specs=in_specs, out_specs=P("ctx", "tp"), check_vma=False)
```

```python
import functools
import math

import jax
import jax.numpy as jnp
from jax import lax
from jax.experimental import pallas as pl
from jax.experimental.pallas import tpu as pltpu
from jax.sharding import PartitionSpec as P

HQ = 32
KVH = 4
HD = 128
ROWS = 128
SEG = 16
BLK = ROWS + SEG
NEG = -1e30
MESH = pl.DeviceIdType.MESH
BF16, F32 = jnp.bfloat16, jnp.float32


def mod4(value):
    return lax.rem(value + 8, 4)


def hadamard_signs():
    both = lax.broadcasted_iota(jnp.int32, (HD, HD), 0) & lax.broadcasted_iota(jnp.int32, (HD, HD), 1)
    both = both ^ (both >> 4)
    both = both ^ (both >> 2)
    both = both ^ (both >> 1)
    return (1 - 2 * (both & 1)).astype(F32).astype(BF16)


def kernel(
    q_ref, mine_ref, seg_ref, w_ref, o_ref,
    kv, wsrc, wb, asrc, ar, osrc, ob, segq, top, den, acc,
    kz_s, kz_r, ka_s, ka_r, kb_s, kb_r, ks_s, ks_r, wz_s, wz_r, wx_s, wx_r, ws_s, ws_r, az_s, az_r, ay_s, ay_r, o_s, o_r,
):
    ctx, tpi = lax.axis_index("ctx"), lax.axis_index("tp")
    h, x, y = lax.div(ctx, 16), lax.rem(lax.div(ctx, 4), 4), lax.rem(ctx, 4)
    z, k = lax.div(tpi, 2), lax.rem(tpi, 2)
    other = 1 - k
    first = x * other + y * k
    second = y * other + x * k

    def device(h_at, x_at, y_at, z_at, core):
        return (mod4(h_at) * 16 + mod4(x_at) * 4 + mod4(y_at), mod4(z_at) * 2 + core)

    def copy(src, dst, send, recv, target):
        return pltpu.make_async_remote_copy(
            src_ref=src, dst_ref=dst, send_sem=send, recv_sem=recv, device_id=target, device_id_type=MESH
        )

    sib = device(h, x, y, z, other)

    barrier = pltpu.get_barrier_semaphore()

    def greet(target):
        pl.semaphore_signal(barrier, inc=1, device_id=target, device_id_type=MESH)

    greet(sib)
    for i in range(1, 4):
        greet(device(h, x + i, y, z, k))
        greet(device(h, x, y + i, z, k))
        greet(device(h, x, y + i, z, other))
        greet(device(h, x, y, z + i, other))

    def greet_line(d, _):
        greet(device(h + lax.div(d, 4), x, y, z + lax.rem(d, 4), k))
        return 0

    lax.fori_loop(1, 16, greet_line, 0)

    kv[k, h, second, first, 0:ROWS, :] = mine_ref[...]
    seg_row = seg_ref[...].astype(F32)
    kv[k, h, second, first, ROWS:BLK, :] = jnp.broadcast_to(seg_row, (SEG, HD)).astype(BF16)
    rotated = jnp.dot(w_ref[...], hadamard_signs(), preferred_element_type=F32) * (1.0 / math.sqrt(HD))
    wsrc[...] = rotated.astype(BF16)
    seg_col = jnp.broadcast_to(seg_row, (ROWS, HD)).T
    for i in range(4):
        segq[i * ROWS : (i + 1) * ROWS, :] = seg_col
    top[...] = jnp.full_like(top, NEG)
    den[...] = jnp.zeros_like(den)
    acc[...] = jnp.zeros_like(acc)

    pl.semaphore_wait(barrier, 28)

    def kv_z(i, out):
        at = kv.at[k, h if out else mod4(h - i), second, first]
        return copy(at, at, kz_s.at[i], kz_r.at[i], device(h + i, x, y, z, k))

    def kv_first(r, i, out):
        at = kv.at[k, mod4(h - r), second, first if out else mod4(first - i)]
        return copy(at, at, ka_s.at[r, i], ka_r.at[r, i], device(h, x + i * other, y + i * k, z, k))

    def kv_second(r, i, out):
        at = kv.at[k, mod4(h - r), second if out else mod4(second - i)]
        return copy(at, at, kb_s.at[r, i], kb_r.at[r, i], device(h, x + i * k, y + i * other, z, k))

    def kv_sib(r, i, out):
        at = kv.at[k if out else other, mod4(h - r), mod4((second if out else first) - i)]
        return copy(at, at, ks_s.at[r, i], ks_r.at[r, i], sib)

    def w_out(i):
        return copy(wsrc, wb.at[k, z, x], wz_s.at[i], wz_r.at[z], device(h + i, x, y, h, k))

    def w_in(j):
        from_z = mod4(z + j)
        at = wb.at[k, from_z, x]
        return copy(at, at, wz_s.at[0], wz_r.at[from_z], device(z, x, y, from_z, k))

    def w_x(j, i, out):
        at = wb.at[k, mod4(z + j), x if out else mod4(x - i)]
        return copy(at, at, wx_s.at[j, i], wx_r.at[j, i], device(h, x + i, y, z, k))

    def w_sib(j, out):
        at = wb.at[k if out else other, mod4(z + j)]
        return copy(at, at, ws_s.at[j], ws_r.at[j], sib)

    def a_z(i, dk, out):
        core = lax.rem(k + dk, 2)
        dst = ar.at[z, k, y] if out else ar.at[mod4(z - i), core, y]
        return copy(asrc.at[core], dst, az_s.at[i, dk], az_r.at[i, dk], device(h, x, y, z + i, core))

    def a_y(i, dy, out):
        at = ar.at[mod4(z - i), :, y if out else mod4(y - dy)]
        return copy(at, at, ay_s.at[i, dy], ay_r.at[i, dy], device(h, x, y + dy, z, k))

    def o_y(dy, dk, out):
        core = lax.rem(k + dk, 2)
        dst = ob.at[k, y] if out else ob.at[core, mod4(y - dy)]
        return copy(osrc.at[mod4(y + dy), core], dst, o_s.at[dy, dk], o_r.at[dy, dk], device(h, x, y + dy, z, core))

    pairs = [(i, dk) for i in range(4) for dk in range(2) if i or dk]

    def first_out(r):
        for i in (2, 1, 3):
            kv_first(r, i, True).start()

    def second_out(r):
        for i in (1, 3, 2):
            kv_first(r, i, False).wait_recv()
        for i in (2, 1, 3):
            kv_second(r, i, True).start()
        kv_sib(r, 0, True).start()

    def sib_out(r):
        for i in (1, 3, 2):
            kv_second(r, i, False).wait_recv()
            kv_sib(r, i, True).start()

    def attend(hp, line, own_plane):
        keys = kv[0, hp, line, :, 0:ROWS, :].reshape(4 * ROWS, HD)
        values = kv[1, hp, :, pl.ds(line, 1), 0:ROWS, :].reshape(4 * ROWS, HD)
        ids = kv[0, hp, line, :, ROWS:BLK, :].astype(F32)
        ids = jnp.concatenate([ids[j, 0:1, :] for j in range(4)], axis=1)
        scores = lax.dot_general(
            q_ref[...], keys, (((1,), (1,)), ((), ())), preferred_element_type=F32
        )
        own = segq[...]
        allowed = ids == jnp.concatenate([own] * 4, axis=1)
        if own_plane:
            lane = lax.broadcasted_iota(jnp.int32, scores.shape, 1)
            place = lane + (lane >> 7) * (3 * ROWS) + line * ROWS
            token = (lax.broadcasted_iota(jnp.int32, scores.shape, 0) & (ROWS - 1)) + (x * 4 + y) * ROWS
            allowed = allowed & (place <= token)
        scores = jnp.where(allowed, scores, NEG)
        before = top[...]
        now = jnp.maximum(before, jnp.max(scores, axis=1, keepdims=True))
        rate = math.log2(math.e) / math.sqrt(HD)
        keep = jnp.exp2((before - now) * rate)
        weights = jnp.exp2((scores - jnp.concatenate([now] * 4, axis=1)) * rate)
        part = (weights[:, 0:128] + weights[:, 128:256]) + (weights[:, 256:384] + weights[:, 384:512])
        top[...] = now
        den[...] = den[...] * keep + part
        acc[...] = acc[...] * keep + jnp.dot(weights.astype(BF16), values, preferred_element_type=F32)

    def attend_plane(r):
        def line(i, _):
            kv_sib(r, i, False).wait_recv()
            return 0

        lax.fori_loop(0, 4, line, 0)

        def lines(i, _):
            attend(mod4(h - r), mod4(y - i), r == 0)
            return 0

        if r == 0:
            lax.fori_loop(0, 4, lines, 0)
        else:

            @pl.when(r <= h)
            def _():
                lax.fori_loop(0, 4, lines, 0)

    for i in (2, 1, 3):
        kv_z(i, True).start()
    first_out(0)
    second_out(0)
    for r in (1, 3):
        kv_z(r, False).wait_recv()
        first_out(r)
    for i in (2, 1, 3):
        w_out(i).start()

    @pl.when(h != z)
    def _():
        w_out(0).start()

    @pl.when(h == z)
    def _():
        wb[k, z, x] = wsrc[...]

    sib_out(0)
    for r in (1, 3):
        second_out(r)
    kv_z(2, False).wait_recv()
    first_out(2)
    sib_out(1)
    second_out(2)
    sib_out(3)

    attend_plane(0)
    attend_plane(1)
    attend_plane(3)
    sib_out(2)
    for j in range(4):
        if j == 0:

            @pl.when(h != z)
            def _():
                w_in(0).wait_recv()
        else:
            w_in(j).wait_recv()
        for i in range(1, 4):
            w_x(j, i, True).start()
    attend_plane(2)

    out = acc[...] / jnp.sum(den[...], axis=1, keepdims=True)
    for head in range(4):
        for half in range(2):
            start = head * ROWS + half * 64
            asrc[half, :, head * HD : (head + 1) * HD] = out[start : start + 64].astype(BF16)
    for i, dk in pairs:
        a_z(i, dk, True).start()
    ar[z, k, y] = asrc[k]
    for i in (0, 1, 3, 2):
        for dk in range(2):
            if i or dk:
                a_z(i, dk, False).wait_recv()
        for dy in (2, 1, 3):
            a_y(i, dy, True).start()

    for j in range(4):
        for i in range(1, 4):
            w_x(j, i, False).wait_recv()
        w_sib(j, True).start()
    for j in range(4):
        w_sib(j, False).wait_recv()

    total = None
    for i in (0, 1, 3, 2):
        for dy in (1, 3, 2):
            a_y(i, dy, False).wait_recv()
        from_z = mod4(z - i)
        for core in range(2):
            rows = ar[from_z, core].reshape(4 * 64, 4 * HD)
            columns = jnp.concatenate([wb[core, from_z, j] for j in range(4)], axis=1)
            term = jnp.dot(rows, columns, preferred_element_type=F32)
            total = term if total is None else total + term

    total = total.astype(BF16)
    for row in range(4):
        for core in range(2):
            for b in range(2):
                col = (core * 2 + b) * HD
                osrc[row, core, b] = total[row * 64 : (row + 1) * 64, col : col + HD]
    for dy, dk in pairs:
        o_y(dy, dk, True).start()
    ob[k, y] = osrc[y, k]
    for dy, dk in pairs:
        o_y(dy, dk, False).wait_recv()
    for core in range(2):
        for row in range(4):
            for b in range(2):
                col = (b * 4 + row) * HD
                o_ref[core * 64 : (core + 1) * 64, col : col + HD] = ob[core, row, b]

    for i in range(1, 4):
        kv_z(i, True).wait_send()
        w_out(i).wait_send()

    @pl.when(h != z)
    def _():
        w_out(0).wait_send()

    for r in range(4):
        for i in range(1, 4):
            kv_first(r, i, True).wait_send()
            kv_second(r, i, True).wait_send()
            w_x(r, i, True).wait_send()
            a_y(r, i, True).wait_send()
        for i in range(4):
            kv_sib(r, i, True).wait_send()
        w_sib(r, True).wait_send()
    for i, dk in pairs:
        a_z(i, dk, True).wait_send()
        o_y(i, dk, True).wait_send()


def body(queries, keys, values, segment_ids, out_weight):
    tpi = lax.axis_index("tp")
    head = tpi // 2
    mine = lax.dynamic_index_in_dim(jnp.where(tpi % 2 == 0, keys, values), head, 1, keepdims=False)
    q_rows = jnp.transpose(queries, (1, 0, 2)).reshape(4 * ROWS, HD)
    dma = pltpu.SemaphoreType.DMA
    return pl.pallas_call(
        kernel,
        out_shape=jax.ShapeDtypeStruct((ROWS, 1024), BF16),
        in_specs=[pl.BlockSpec(memory_space=pltpu.VMEM)] * 4,
        out_specs=pl.BlockSpec(memory_space=pltpu.VMEM),
        scratch_shapes=[
            pltpu.VMEM((2, 4, 4, 4, BLK, HD), BF16),
            pltpu.VMEM((512, HD), BF16),
            pltpu.VMEM((2, 4, 4, 512, HD), BF16),
            pltpu.VMEM((2, 64, 512), BF16),
            pltpu.VMEM((4, 2, 4, 64, 512), BF16),
            pltpu.VMEM((4, 2, 2, 64, HD), BF16),
            pltpu.VMEM((2, 4, 2, 64, HD), BF16),
            pltpu.VMEM((512, HD), F32),
            pltpu.VMEM((512, HD), F32),
            pltpu.VMEM((512, HD), F32),
            pltpu.VMEM((512, HD), F32),
        ]
        + [dma((4,))] * 2
        + [dma((4, 4))] * 6
        + [dma((4,))] * 2
        + [dma((4, 4))] * 2
        + [dma((4,))] * 2
        + [dma((4, 2))] * 2
        + [dma((4, 4))] * 2
        + [dma((4, 2))] * 2,
        compiler_params=pltpu.CompilerParams(
            collective_id=0, has_side_effects=True, vmem_limit_bytes=48 << 20
        ),
        name="attention_projection",
    )(q_rows, mine, segment_ids.reshape(1, ROWS), out_weight)


def solution(mesh):
    in_specs = (
        P("ctx", "tp", None),
        P("ctx", None, None),
        P("ctx", None, None),
        P("ctx"),
        P("tp", "ctx"),
    )
    return jax.shard_map(body, mesh=mesh, in_specs=in_specs, out_specs=P("ctx", "tp"), check_vma=False)
```

```python
import functools
import math

import jax
import jax.numpy as jnp
from jax import lax
from jax.experimental import pallas as pl
from jax.experimental.pallas import tpu as pltpu
from jax.sharding import PartitionSpec as P

HQ = 32
KVH = 4
HD = 128
ROWS = 128
SEG = 16
BLK = ROWS + SEG
NEG = -1e30
MESH = pl.DeviceIdType.MESH
BF16, F32 = jnp.bfloat16, jnp.float32


def mod4(value):
    return lax.rem(value + 8, 4)


def hadamard_signs():
    both = lax.broadcasted_iota(jnp.int32, (HD, HD), 0) & lax.broadcasted_iota(jnp.int32, (HD, HD), 1)
    both = both ^ (both >> 4)
    both = both ^ (both >> 2)
    both = both ^ (both >> 1)
    return (1 - 2 * (both & 1)).astype(F32).astype(BF16)


def kernel(
    q_ref, mine_ref, seg_ref, w_ref, o_ref,
    kv, wsrc, wb, asrc, ar, osrc, ob, segq, top, den, acc,
    kz_s, kz_r, ka_s, ka_r, kb_s, kb_r, ks_s, ks_r, wz_s, wz_r, wx_s, wx_r, ws_s, ws_r, az_s, az_r, ay_s, ay_r, o_s, o_r,
):
    ctx, tpi = lax.axis_index("ctx"), lax.axis_index("tp")
    h, x, y = lax.div(ctx, 16), lax.rem(lax.div(ctx, 4), 4), lax.rem(ctx, 4)
    z, k = lax.div(tpi, 2), lax.rem(tpi, 2)
    other = 1 - k
    first = x * other + y * k
    second = y * other + x * k

    def device(h_at, x_at, y_at, z_at, core):
        return (mod4(h_at) * 16 + mod4(x_at) * 4 + mod4(y_at), mod4(z_at) * 2 + core)

    def copy(src, dst, send, recv, target):
        return pltpu.make_async_remote_copy(
            src_ref=src, dst_ref=dst, send_sem=send, recv_sem=recv, device_id=target, device_id_type=MESH
        )

    sib = device(h, x, y, z, other)

    barrier = pltpu.get_barrier_semaphore()

    def greet(target):
        pl.semaphore_signal(barrier, inc=1, device_id=target, device_id_type=MESH)

    greet(sib)
    for i in range(1, 4):
        greet(device(h, x + i, y, z, k))
        greet(device(h, x, y + i, z, k))
        greet(device(h, x, y + i, z, other))
        greet(device(h, x, y, z + i, other))

    def greet_line(d, _):
        greet(device(h + lax.div(d, 4), x, y, z + lax.rem(d, 4), k))
        return 0

    lax.fori_loop(1, 16, greet_line, 0)

    kv[k, h, second, first, 0:ROWS, :] = mine_ref[...]
    seg_row = seg_ref[...].astype(F32)
    kv[k, h, second, first, ROWS:BLK, :] = jnp.broadcast_to(seg_row, (SEG, HD)).astype(BF16)
    rotated = jnp.dot(w_ref[...], hadamard_signs(), preferred_element_type=F32) * (1.0 / math.sqrt(HD))
    wsrc[...] = rotated.astype(BF16)
    seg_col = jnp.broadcast_to(seg_row, (ROWS, HD)).T
    for i in range(4):
        segq[i * ROWS : (i + 1) * ROWS, :] = seg_col
    top[...] = jnp.full_like(top, NEG)
    den[...] = jnp.zeros_like(den)
    acc[...] = jnp.zeros_like(acc)

    pl.semaphore_wait(barrier, 28)

    def kv_z(i, out):
        at = kv.at[k, h if out else mod4(h - i), second, first]
        return copy(at, at, kz_s.at[i], kz_r.at[i], device(h + i, x, y, z, k))

    def kv_first(r, i, out):
        at = kv.at[k, mod4(h - r), second, first if out else mod4(first - i)]
        return copy(at, at, ka_s.at[r, i], ka_r.at[r, i], device(h, x + i * other, y + i * k, z, k))

    def kv_second(r, i, out):
        at = kv.at[k, mod4(h - r), second if out else mod4(second - i)]
        return copy(at, at, kb_s.at[r, i], kb_r.at[r, i], device(h, x + i * k, y + i * other, z, k))

    def kv_sib(r, i, out):
        at = kv.at[k if out else other, mod4(h - r), mod4((second if out else first) - i)]
        return copy(at, at, ks_s.at[r, i], ks_r.at[r, i], sib)

    def depth(c):
        return pl.ds(c * 256, 256)

    def w_out(i, c):
        dst = wb.at[k, z, x, depth(c)]
        return copy(wsrc.at[depth(c)], dst, wz_s.at[c, i], wz_r.at[c, z], device(h + i, x, y, h, k))

    def w_in(j, c):
        from_z = mod4(z + j)
        at = wb.at[k, from_z, x, depth(c)]
        return copy(at, at, wz_s.at[c, 0], wz_r.at[c, from_z], device(z, x, y, from_z, k))

    def w_x(j, i, c, out):
        at = wb.at[k, mod4(z + j), x if out else mod4(x - i), depth(c)]
        return copy(at, at, wx_s.at[c, j, i], wx_r.at[c, j, i], device(h, x + i, y, z, k))

    def w_sib(j, c, out):
        at = wb.at[k if out else other, mod4(z + j), :, depth(c)]
        return copy(at, at, ws_s.at[c, j], ws_r.at[c, j], sib)

    def a_z(i, dk, out):
        core = lax.rem(k + dk, 2)
        dst = ar.at[z, k, y] if out else ar.at[mod4(z - i), core, y]
        return copy(asrc.at[core], dst, az_s.at[i, dk], az_r.at[i, dk], device(h, x, y, z + i, core))

    def a_y(i, dy, out):
        at = ar.at[mod4(z - i), :, y if out else mod4(y - dy)]
        return copy(at, at, ay_s.at[i, dy], ay_r.at[i, dy], device(h, x, y + dy, z, k))

    def o_y(dy, dk, out):
        core = lax.rem(k + dk, 2)
        dst = ob.at[k, y] if out else ob.at[core, mod4(y - dy)]
        return copy(osrc.at[mod4(y + dy), core], dst, o_s.at[dy, dk], o_r.at[dy, dk], device(h, x, y + dy, z, core))

    pairs = [(i, dk) for i in range(4) for dk in range(2) if i or dk]

    def first_out(r):
        for i in (2, 1, 3):
            kv_first(r, i, True).start()

    def second_out(r):
        for i in (1, 3, 2):
            kv_first(r, i, False).wait_recv()
        for i in (2, 1, 3):
            kv_second(r, i, True).start()
        kv_sib(r, 0, True).start()

    def sib_out(r):
        for i in (1, 3, 2):
            kv_second(r, i, False).wait_recv()
            kv_sib(r, i, True).start()

    def attend(hp, line, own_plane):
        keys = kv[0, hp, line, :, 0:ROWS, :].reshape(4 * ROWS, HD)
        values = kv[1, hp, :, pl.ds(line, 1), 0:ROWS, :].reshape(4 * ROWS, HD)
        ids = kv[0, hp, line, :, ROWS:BLK, :].astype(F32)
        ids = jnp.concatenate([ids[j, 0:1, :] for j in range(4)], axis=1)
        scores = lax.dot_general(
            q_ref[...], keys, (((1,), (1,)), ((), ())), preferred_element_type=F32
        )
        own = segq[...]
        allowed = ids == jnp.concatenate([own] * 4, axis=1)
        if own_plane:
            lane = lax.broadcasted_iota(jnp.int32, scores.shape, 1)
            place = lane + (lane >> 7) * (3 * ROWS) + line * ROWS
            token = (lax.broadcasted_iota(jnp.int32, scores.shape, 0) & (ROWS - 1)) + (x * 4 + y) * ROWS
            allowed = allowed & (place <= token)
        scores = jnp.where(allowed, scores, NEG)
        before = top[...]
        now = jnp.maximum(before, jnp.max(scores, axis=1, keepdims=True))
        rate = math.log2(math.e) / math.sqrt(HD)
        keep = jnp.exp2((before - now) * rate)
        weights = jnp.exp2((scores - jnp.concatenate([now] * 4, axis=1)) * rate)
        part = (weights[:, 0:128] + weights[:, 128:256]) + (weights[:, 256:384] + weights[:, 384:512])
        top[...] = now
        den[...] = den[...] * keep + part
        acc[...] = acc[...] * keep + jnp.dot(weights.astype(BF16), values, preferred_element_type=F32)

    def attend_plane(r):
        def line(i, _):
            kv_sib(r, i, False).wait_recv()
            return 0

        lax.fori_loop(0, 4, line, 0)

        def lines(i, _):
            attend(mod4(h - r), mod4(y - i), r == 0)
            return 0

        if r == 0:
            lax.fori_loop(0, 4, lines, 0)
        else:

            @pl.when(r <= h)
            def _():
                lax.fori_loop(0, 4, lines, 0)

    for i in (2, 1, 3):
        kv_z(i, True).start()
    first_out(0)
    second_out(0)
    for r in (1, 3, 2):
        kv_z(r, False).wait_recv()
        first_out(r)
    for c in range(2):
        for i in (2, 1, 3):
            w_out(i, c).start()

        @pl.when(h != z)
        def _(c=c):
            w_out(0, c).start()

    @pl.when(h == z)
    def _():
        wb[k, z, x] = wsrc[...]

    for r in (1, 3, 2):
        second_out(r)

    def w_on(j, c):
        if j == 0:

            @pl.when(h != z)
            def _():
                w_in(0, c).wait_recv()
        else:
            w_in(j, c).wait_recv()
        for i in (2, 1, 3):
            w_x(j, i, c, True).start()

    sib_out(0)
    attend_plane(0)
    sib_out(1)
    attend_plane(1)
    sib_out(3)
    attend_plane(3)
    sib_out(2)
    attend_plane(2)

    out = acc[...] / jnp.sum(den[...], axis=1, keepdims=True)
    for head in range(4):
        for half in range(2):
            start = head * ROWS + half * 64
            asrc[half, :, head * HD : (head + 1) * HD] = out[start : start + 64].astype(BF16)
    for i, dk in pairs:
        a_z(i, dk, True).start()
    ar[z, k, y] = asrc[k]
    for j in range(4):
        w_on(j, 0)

    def a_on(i):
        for dk in range(2):
            if i or dk:
                a_z(i, dk, False).wait_recv()
        for dy in (2, 1, 3):
            a_y(i, dy, True).start()

    a_on(0)
    for r in (1, 3, 2):
        w_on({1:0,3:1,2:2}[r], 1)
        a_on(r)
    w_on(3, 1)

    for c in range(2):
        for j in range(4):
            for i in range(1, 4):
                w_x(j, i, c, False).wait_recv()
            w_sib(j, c, True).start()
    for c in range(2):
        for j in range(4):
            w_sib(j, c, False).wait_recv()

    total = None
    for i in (0, 1, 3, 2):
        for dy in (1, 3, 2):
            a_y(i, dy, False).wait_recv()
        from_z = mod4(z - i)
        for core in range(2):
            rows = ar[from_z, core].reshape(4 * 64, 4 * HD)
            columns = jnp.concatenate([wb[core, from_z, j] for j in range(4)], axis=1)
            term = jnp.dot(rows, columns, preferred_element_type=F32)
            total = term if total is None else total + term

    total = total.astype(BF16)
    for row in range(4):
        for core in range(2):
            for b in range(2):
                col = (core * 2 + b) * HD
                osrc[row, core, b] = total[row * 64 : (row + 1) * 64, col : col + HD]
    for dy, dk in pairs:
        o_y(dy, dk, True).start()
    ob[k, y] = osrc[y, k]
    for dy, dk in pairs:
        o_y(dy, dk, False).wait_recv()
    for core in range(2):
        for row in range(4):
            for b in range(2):
                col = (b * 4 + row) * HD
                o_ref[core * 64 : (core + 1) * 64, col : col + HD] = ob[core, row, b]

    for i in range(1, 4):
        kv_z(i, True).wait_send()
        for c in range(2):
            w_out(i, c).wait_send()

    @pl.when(h != z)
    def _():
        for c in range(2):
            w_out(0, c).wait_send()

    for r in range(4):
        for i in range(1, 4):
            kv_first(r, i, True).wait_send()
            kv_second(r, i, True).wait_send()
            for c in range(2):
                w_x(r, i, c, True).wait_send()
            a_y(r, i, True).wait_send()
        for i in range(4):
            kv_sib(r, i, True).wait_send()
        for c in range(2):
            w_sib(r, c, True).wait_send()
    for i, dk in pairs:
        a_z(i, dk, True).wait_send()
        o_y(i, dk, True).wait_send()


def body(queries, keys, values, segment_ids, out_weight):
    tpi = lax.axis_index("tp")
    head = tpi // 2
    mine = lax.dynamic_index_in_dim(jnp.where(tpi % 2 == 0, keys, values), head, 1, keepdims=False)
    q_rows = jnp.transpose(queries, (1, 0, 2)).reshape(4 * ROWS, HD)
    dma = pltpu.SemaphoreType.DMA
    return pl.pallas_call(
        kernel,
        out_shape=jax.ShapeDtypeStruct((ROWS, 1024), BF16),
        in_specs=[pl.BlockSpec(memory_space=pltpu.VMEM)] * 4,
        out_specs=pl.BlockSpec(memory_space=pltpu.VMEM),
        scratch_shapes=[
            pltpu.VMEM((2, 4, 4, 4, BLK, HD), BF16),
            pltpu.VMEM((512, HD), BF16),
            pltpu.VMEM((2, 4, 4, 512, HD), BF16),
            pltpu.VMEM((2, 64, 512), BF16),
            pltpu.VMEM((4, 2, 4, 64, 512), BF16),
            pltpu.VMEM((4, 2, 2, 64, HD), BF16),
            pltpu.VMEM((2, 4, 2, 64, HD), BF16),
            pltpu.VMEM((512, HD), F32),
            pltpu.VMEM((512, HD), F32),
            pltpu.VMEM((512, HD), F32),
            pltpu.VMEM((512, HD), F32),
        ]
        + [dma((4,))] * 2
        + [dma((4, 4))] * 6
        + [dma((2, 4))] * 2
        + [dma((2, 4, 4))] * 2
        + [dma((2, 4))] * 2
        + [dma((4, 2))] * 2
        + [dma((4, 4))] * 2
        + [dma((4, 2))] * 2,
        compiler_params=pltpu.CompilerParams(
            collective_id=0, has_side_effects=True, vmem_limit_bytes=48 << 20
        ),
        name="attention_projection",
    )(q_rows, mine, segment_ids.reshape(1, ROWS), out_weight)


def solution(mesh):
    in_specs = (
        P("ctx", "tp", None),
        P("ctx", None, None),
        P("ctx", None, None),
        P("ctx"),
        P("tp", "ctx"),
    )
    return jax.shard_map(body, mesh=mesh, in_specs=in_specs, out_specs=P("ctx", "tp"), check_vma=False)
```

```python
import functools
import math

import jax
import jax.numpy as jnp
from jax import lax
from jax.experimental import pallas as pl
from jax.experimental.pallas import tpu as pltpu
from jax.sharding import PartitionSpec as P

HQ = 32
KVH = 4
HD = 128
ROWS = 128
SEG = 16
BLK = ROWS + SEG
NEG = -1e30
MESH = pl.DeviceIdType.MESH
BF16, F32 = jnp.bfloat16, jnp.float32


def mod4(value):
    return lax.rem(value + 8, 4)


def hadamard_signs():
    both = lax.broadcasted_iota(jnp.int32, (HD, HD), 0) & lax.broadcasted_iota(jnp.int32, (HD, HD), 1)
    both = both ^ (both >> 4)
    both = both ^ (both >> 2)
    both = both ^ (both >> 1)
    return (1 - 2 * (both & 1)).astype(F32).astype(BF16)


def kernel(
    q_in, k_in, v_in, seg_in, w_in_hbm, o_ref,
    q_raw, kv_raw, seg_ref, w_ref, q_ref, in_sem,
    kv, wsrc, wb, asrc, ar, osrc, ob, segq, top, den, acc,
    kz_s, kz_r, ka_s, ka_r, kb_s, kb_r, ks_s, ks_r, wz_s, wz_r, wx_s, wx_r, ws_s, ws_r, az_s, az_r, ay_s, ay_r, o_s, o_r,
):
    ctx, tpi = lax.axis_index("ctx"), lax.axis_index("tp")
    h, x, y = lax.div(ctx, 16), lax.rem(lax.div(ctx, 4), 4), lax.rem(ctx, 4)
    z, k = lax.div(tpi, 2), lax.rem(tpi, 2)
    other = 1 - k
    first = x * other + y * k
    second = y * other + x * k

    def device(h_at, x_at, y_at, z_at, core):
        return (mod4(h_at) * 16 + mod4(x_at) * 4 + mod4(y_at), mod4(z_at) * 2 + core)

    def copy(src, dst, send, recv, target):
        return pltpu.make_async_remote_copy(
            src_ref=src, dst_ref=dst, send_sem=send, recv_sem=recv, device_id=target, device_id_type=MESH
        )

    sib = device(h, x, y, z, other)

    def load(src, dst, i):
        return pltpu.make_async_copy(src, dst, in_sem.at[i])

    @pl.when(k == 0)
    def _():
        load(k_in, kv_raw, 0).start()

    @pl.when(k == 1)
    def _():
        load(v_in, kv_raw, 0).start()

    load(seg_in, seg_ref, 1).start()
    load(w_in_hbm, w_ref, 2).start()
    load(q_in, q_raw, 3).start()

    barrier = pltpu.get_barrier_semaphore()

    def greet(target):
        pl.semaphore_signal(barrier, inc=1, device_id=target, device_id_type=MESH)

    greet(sib)
    for i in range(1, 4):
        greet(device(h, x + i, y, z, k))
        greet(device(h, x, y + i, z, k))
        greet(device(h, x, y + i, z, other))
        greet(device(h, x, y, z + i, other))

    def greet_line(d, _):
        greet(device(h + lax.div(d, 4), x, y, z + lax.rem(d, 4), k))
        return 0

    lax.fori_loop(1, 16, greet_line, 0)

    load(k_in, kv_raw, 0).wait()
    by_head = kv_raw[...].astype(F32)
    for head in range(KVH):

        @pl.when(z == head)
        def _(head=head):
            kv[k, h, second, first, 0:ROWS, :] = by_head[:, head, :].astype(BF16)

    load(seg_in, seg_ref, 1).wait()
    seg_row = seg_ref[...].astype(F32)
    kv[k, h, second, first, ROWS:BLK, :] = jnp.broadcast_to(seg_row, (SEG, HD)).astype(BF16)
    load(w_in_hbm, w_ref, 2).wait()
    rotated = jnp.dot(w_ref[...], hadamard_signs(), preferred_element_type=F32) * (1.0 / math.sqrt(HD))
    wsrc[...] = rotated.astype(BF16)
    load(q_in, q_raw, 3).wait()
    by_head = q_raw[...].astype(F32)
    for head in range(4):
        q_ref[head * ROWS : (head + 1) * ROWS, :] = by_head[:, head, :].astype(BF16)
    seg_col = jnp.broadcast_to(seg_row, (ROWS, HD)).T
    for i in range(4):
        segq[i * ROWS : (i + 1) * ROWS, :] = seg_col
    top[...] = jnp.full_like(top, NEG)
    den[...] = jnp.zeros_like(den)
    acc[...] = jnp.zeros_like(acc)

    pl.semaphore_wait(barrier, 28)

    def kv_z(i, out):
        at = kv.at[k, h if out else mod4(h - i), second, first]
        return copy(at, at, kz_s.at[i], kz_r.at[i], device(h + i, x, y, z, k))

    def kv_first(r, i, out):
        at = kv.at[k, mod4(h - r), second, first if out else mod4(first - i)]
        return copy(at, at, ka_s.at[r, i], ka_r.at[r, i], device(h, x + i * other, y + i * k, z, k))

    def kv_second(r, i, out):
        at = kv.at[k, mod4(h - r), second if out else mod4(second - i)]
        return copy(at, at, kb_s.at[r, i], kb_r.at[r, i], device(h, x + i * k, y + i * other, z, k))

    def kv_sib(r, i, out):
        at = kv.at[k if out else other, mod4(h - r), mod4((second if out else first) - i)]
        return copy(at, at, ks_s.at[r, i], ks_r.at[r, i], sib)

    def depth(c):
        return pl.ds(c * 256, 256)

    def w_out(to, c):
        dst = wb.at[k, z, x, depth(c)]
        return copy(wsrc.at[depth(c)], dst, wz_s.at[c, to], wz_r.at[c, z], device(to, x, y, h, k))

    def w_remote(to):
        return (h != to) | (z != h)

    def w_in(j, c):
        from_z = mod4(z + j)
        at = wb.at[k, from_z, x, depth(c)]
        return copy(at, at, wz_s.at[c, 0], wz_r.at[c, from_z], device(z, x, y, from_z, k))

    def w_x(j, i, c, out):
        at = wb.at[k, mod4(z + j), x if out else mod4(x - i), depth(c)]
        return copy(at, at, wx_s.at[c, j, i], wx_r.at[c, j, i], device(h, x + i, y, z, k))

    def w_sib(j, c, out):
        at = wb.at[k if out else other, mod4(z + j), :, depth(c)]
        return copy(at, at, ws_s.at[c, j], ws_r.at[c, j], sib)

    def a_z(i, dk, out):
        core = lax.rem(k + dk, 2)
        dst = ar.at[z, k, y] if out else ar.at[mod4(z - i), core, y]
        return copy(asrc.at[core], dst, az_s.at[i, dk], az_r.at[i, dk], device(h, x, y, z + i, core))

    def a_y(i, dy, out):
        at = ar.at[mod4(z - i), :, y if out else mod4(y - dy)]
        return copy(at, at, ay_s.at[i, dy], ay_r.at[i, dy], device(h, x, y + dy, z, k))

    def o_y(dy, dk, out):
        core = lax.rem(k + dk, 2)
        dst = ob.at[k, y] if out else ob.at[core, mod4(y - dy)]
        return copy(osrc.at[mod4(y + dy), core], dst, o_s.at[dy, dk], o_r.at[dy, dk], device(h, x, y + dy, z, core))

    pairs = [(i, dk) for i in range(4) for dk in range(2) if i or dk]

    def first_out(r):
        for i in (2, 1, 3):
            kv_first(r, i, True).start()

    def second_out(r):
        for i in (1, 3, 2):
            kv_first(r, i, False).wait_recv()
        for i in (2, 1, 3):
            kv_second(r, i, True).start()
        kv_sib(r, 0, True).start()

    def sib_out(r):
        for i in (1, 3, 2):
            kv_second(r, i, False).wait_recv()
            kv_sib(r, i, True).start()

    def attend(hp, line, own_plane):
        keys = kv[0, hp, line, :, 0:ROWS, :].reshape(4 * ROWS, HD)
        values = kv[1, hp, :, pl.ds(line, 1), 0:ROWS, :].reshape(4 * ROWS, HD)
        ids = kv[0, hp, line, :, ROWS:BLK, :].astype(F32)
        ids = jnp.concatenate([ids[j, 0:1, :] for j in range(4)], axis=1)
        scores = lax.dot_general(
            q_ref[...], keys, (((1,), (1,)), ((), ())), preferred_element_type=F32
        )
        own = segq[...]
        allowed = ids == jnp.concatenate([own] * 4, axis=1)
        if own_plane:
            lane = lax.broadcasted_iota(jnp.int32, scores.shape, 1)
            place = lane + (lane >> 7) * (3 * ROWS) + line * ROWS
            token = (lax.broadcasted_iota(jnp.int32, scores.shape, 0) & (ROWS - 1)) + (x * 4 + y) * ROWS
            allowed = allowed & (place <= token)
        scores = jnp.where(allowed, scores, NEG)
        before = top[...]
        now = jnp.maximum(before, jnp.max(scores, axis=1, keepdims=True))
        rate = math.log2(math.e) / math.sqrt(HD)
        keep = jnp.exp2((before - now) * rate)
        weights = jnp.exp2((scores - jnp.concatenate([now] * 4, axis=1)) * rate)
        part = (weights[:, 0:128] + weights[:, 128:256]) + (weights[:, 256:384] + weights[:, 384:512])
        top[...] = now
        den[...] = den[...] * keep + part
        acc[...] = acc[...] * keep + jnp.dot(weights.astype(BF16), values, preferred_element_type=F32)

    def attend_plane(r):
        def line(i, _):
            kv_sib(r, i, False).wait_recv()
            return 0

        lax.fori_loop(0, 4, line, 0)

        def lines(i, _):
            attend(mod4(h - r), mod4(y - i), r == 0)
            return 0

        lax.fori_loop(0, 4, lines, 0)

    def w_start(to, also=True, parts=(0, 1)):
        @pl.when(w_remote(to) & also)
        def _():
            for c in parts:
                w_out(to, c).start()

    def later(r, step):
        @pl.when(r <= h)
        def _():
            step(r)

    def passed_on(r):
        kv_z(r, False).wait_recv()
        first_out(r)

    for i in (2, 1, 3):

        @pl.when(h + i <= 3)
        def _(i=i):
            kv_z(i, True).start()

    first_out(0)
    second_out(0)
    for r in (1, 3):
        later(r, passed_on)
    w_start(0)
    w_start(1, h > 0)
    for to in range(1, 4):
        w_start(to, h == 0, (0,))
    later(2, passed_on)

    @pl.when(h == z)
    def _():
        wb[k, z, x] = wsrc[...]

    for r in (1, 3, 2):
        later(r, second_out)
    w_start(2, h > 0)
    w_start(3, h > 0)

    def w_on(j, c):
        if j == 0:

            @pl.when(h != z)
            def _():
                w_in(0, c).wait_recv()
        else:
            w_in(j, c).wait_recv()
        for i in (2, 1, 3):
            w_x(j, i, c, True).start()

    sib_out(0)
    attend_plane(0)
    for r in (1, 3, 2):
        later(r, sib_out)
        later(r, attend_plane)

    out = acc[...] / jnp.sum(den[...], axis=1, keepdims=True)
    for head in range(4):
        for half in range(2):
            start = head * ROWS + half * 64
            asrc[half, :, head * HD : (head + 1) * HD] = out[start : start + 64].astype(BF16)
    for i, dk in pairs:
        a_z(i, dk, True).start()
    ar[z, k, y] = asrc[k]
    for to in range(1, 4):
        w_start(to, h == 0, (1,))
    for j in range(4):
        w_on(j, 0)

    def a_on(i):
        for dk in range(2):
            if i or dk:
                a_z(i, dk, False).wait_recv()
        for dy in (2, 1, 3):
            a_y(i, dy, True).start()

    a_on(0)
    for r in (1, 3, 2):
        w_on({1:0,3:1,2:2}[r], 1)
        a_on(r)
    w_on(3, 1)

    for c in range(2):
        for j in range(4):
            for i in range(1, 4):
                w_x(j, i, c, False).wait_recv()
            w_sib(j, c, True).start()
    for c in range(2):
        for j in range(4):
            w_sib(j, c, False).wait_recv()

    total = None
    for i in (0, 1, 3, 2):
        for dy in (1, 3, 2):
            a_y(i, dy, False).wait_recv()
        from_z = mod4(z - i)
        for core in range(2):
            rows = ar[from_z, core].reshape(4 * 64, 4 * HD)
            columns = jnp.concatenate([wb[core, from_z, j] for j in range(4)], axis=1)
            term = jnp.dot(rows, columns, preferred_element_type=F32)
            total = term if total is None else total + term

    total = total.astype(BF16)
    for row in range(4):
        for core in range(2):
            for b in range(2):
                col = (core * 2 + b) * HD
                osrc[row, core, b] = total[row * 64 : (row + 1) * 64, col : col + HD]
    for dy, dk in pairs:
        o_y(dy, dk, True).start()
    ob[k, y] = osrc[y, k]
    for dy, dk in pairs:
        o_y(dy, dk, False).wait_recv()
    for core in range(2):
        for row in range(4):
            for b in range(2):
                col = (b * 4 + row) * HD
                o_ref[core * 64 : (core + 1) * 64, col : col + HD] = ob[core, row, b]

    def kv_left(r):
        for i in range(1, 4):
            kv_first(r, i, True).wait_send()
            kv_second(r, i, True).wait_send()
        for i in range(4):
            kv_sib(r, i, True).wait_send()

    kv_left(0)
    for r in range(1, 4):
        later(r, kv_left)

        @pl.when(h + r <= 3)
        def _(r=r):
            kv_z(r, True).wait_send()

    for r in range(4):

        @pl.when(w_remote(r))
        def _(r=r):
            for c in range(2):
                w_out(r, c).wait_send()

        for i in range(1, 4):
            a_y(r, i, True).wait_send()
            for c in range(2):
                w_x(r, i, c, True).wait_send()
        for c in range(2):
            w_sib(r, c, True).wait_send()
    for i, dk in pairs:
        a_z(i, dk, True).wait_send()
        o_y(i, dk, True).wait_send()


def body(queries, keys, values, segment_ids, out_weight):
    dma = pltpu.SemaphoreType.DMA
    return pl.pallas_call(
        kernel,
        out_shape=jax.ShapeDtypeStruct((ROWS, 1024), BF16),
        in_specs=[pl.BlockSpec(memory_space=pl.ANY)] * 5,
        out_specs=pl.BlockSpec(memory_space=pltpu.VMEM),
        scratch_shapes=[
            pltpu.VMEM((ROWS, 4, HD), BF16),
            pltpu.VMEM((ROWS, KVH, HD), BF16),
            pltpu.VMEM((1, ROWS), jnp.int32),
            pltpu.VMEM((512, HD), BF16),
            pltpu.VMEM((512, HD), BF16),
            dma((4,)),
            pltpu.VMEM((2, 4, 4, 4, BLK, HD), BF16),
            pltpu.VMEM((512, HD), BF16),
            pltpu.VMEM((2, 4, 4, 512, HD), BF16),
            pltpu.VMEM((2, 64, 512), BF16),
            pltpu.VMEM((4, 2, 4, 64, 512), BF16),
            pltpu.VMEM((4, 2, 2, 64, HD), BF16),
            pltpu.VMEM((2, 4, 2, 64, HD), BF16),
            pltpu.VMEM((512, HD), F32),
            pltpu.VMEM((512, HD), F32),
            pltpu.VMEM((512, HD), F32),
            pltpu.VMEM((512, HD), F32),
        ]
        + [dma((4,))] * 2
        + [dma((4, 4))] * 6
        + [dma((2, 4))] * 2
        + [dma((2, 4, 4))] * 2
        + [dma((2, 4))] * 2
        + [dma((4, 2))] * 2
        + [dma((4, 4))] * 2
        + [dma((4, 2))] * 2,
        compiler_params=pltpu.CompilerParams(
            collective_id=0, has_side_effects=True, vmem_limit_bytes=60 << 20
        ),
        name="attention_projection",
    )(queries, keys, values, segment_ids.reshape(1, ROWS), out_weight)


def solution(mesh):
    in_specs = (
        P("ctx", "tp", None),
        P("ctx", None, None),
        P("ctx", None, None),
        P("ctx"),
        P("tp", "ctx"),
    )
    return jax.shard_map(body, mesh=mesh, in_specs=in_specs, out_specs=P("ctx", "tp"), check_vma=False)
```

```python
import functools
import math

import jax
import jax.numpy as jnp
from jax import lax
from jax.experimental import pallas as pl
from jax.experimental.pallas import tpu as pltpu
from jax.sharding import PartitionSpec as P

HQ = 32
KVH = 4
HD = 128
ROWS = 128
SEG = 16
BLK = ROWS + SEG
NEG = -1e30
MESH = pl.DeviceIdType.MESH
BF16, F32 = jnp.bfloat16, jnp.float32


def mod4(value):
    return lax.rem(value + 8, 4)


def hadamard_signs():
    both = lax.broadcasted_iota(jnp.int32, (HD, HD), 0) & lax.broadcasted_iota(jnp.int32, (HD, HD), 1)
    both = both ^ (both >> 4)
    both = both ^ (both >> 2)
    both = both ^ (both >> 1)
    return (1 - 2 * (both & 1)).astype(F32).astype(BF16)


def kernel(
    q_in, k_in, v_in, seg_in, w_in_hbm, o_ref,
    q_raw, kv_raw, seg_ref, w_ref, q_ref, in_sem,
    kv, wsrc, wb, asrc, ar, osrc, ob, segq, top, den, acc,
    kz_s, kz_r, ka_s, ka_r, kb_s, kb_r, ks_s, ks_r, wz_s, wz_r, wx_s, wx_r, ws_s, ws_r, az_s, az_r, ay_s, ay_r, o_s, o_r,
):
    ctx, tpi = lax.axis_index("ctx"), lax.axis_index("tp")
    h, x, y = lax.div(ctx, 16), lax.rem(lax.div(ctx, 4), 4), lax.rem(ctx, 4)
    z, k = lax.div(tpi, 2), lax.rem(tpi, 2)
    other = 1 - k
    first = x * other + y * k
    second = y * other + x * k

    def device(h_at, x_at, y_at, z_at, core):
        return (mod4(h_at) * 16 + mod4(x_at) * 4 + mod4(y_at), mod4(z_at) * 2 + core)

    def copy(src, dst, send, recv, target):
        return pltpu.make_async_remote_copy(
            src_ref=src, dst_ref=dst, send_sem=send, recv_sem=recv, device_id=target, device_id_type=MESH
        )

    sib = device(h, x, y, z, other)

    def load(src, dst, i):
        return pltpu.make_async_copy(src, dst, in_sem.at[i])

    @pl.when(k == 0)
    def _():
        load(k_in, kv_raw, 0).start()

    @pl.when(k == 1)
    def _():
        load(v_in, kv_raw, 0).start()

    load(seg_in, seg_ref, 1).start()
    load(w_in_hbm, w_ref, 2).start()
    load(q_in, q_raw, 3).start()

    barrier = pltpu.get_barrier_semaphore()

    def greet(target):
        pl.semaphore_signal(barrier, inc=1, device_id=target, device_id_type=MESH)

    greet(sib)
    for i in range(1, 4):
        greet(device(h, x + i, y, z, k))
        greet(device(h, x, y + i, z, k))
        greet(device(h, x, y + i, z, other))
        greet(device(h, x, y, z + i, other))

    def greet_line(d, _):
        greet(device(h + lax.div(d, 4), x, y, z + lax.rem(d, 4), k))
        return 0

    lax.fori_loop(1, 16, greet_line, 0)

    load(k_in, kv_raw, 0).wait()
    by_head = kv_raw[...].astype(F32)
    for head in range(KVH):

        @pl.when(z == head)
        def _(head=head):
            kv[k, h, second, first, 0:ROWS, :] = by_head[:, head, :].astype(BF16)

    load(seg_in, seg_ref, 1).wait()
    seg_row = seg_ref[...].astype(F32)
    kv[k, h, second, first, ROWS:BLK, :] = jnp.broadcast_to(seg_row, (SEG, HD)).astype(BF16)
    pl.semaphore_wait(barrier, 28)

    def kv_z(i, out):
        at = kv.at[k, h if out else mod4(h - i), second, first]
        return copy(at, at, kz_s.at[i], kz_r.at[i], device(h + i, x, y, z, k))

    def kv_first(r, i, out):
        at = kv.at[k, mod4(h - r), second, first if out else mod4(first - i)]
        return copy(at, at, ka_s.at[r, i], ka_r.at[r, i], device(h, x + i * other, y + i * k, z, k))

    def kv_second(r, i, out):
        at = kv.at[k, mod4(h - r), second if out else mod4(second - i)]
        return copy(at, at, kb_s.at[r, i], kb_r.at[r, i], device(h, x + i * k, y + i * other, z, k))

    def kv_sib(r, i, out):
        at = kv.at[k if out else other, mod4(h - r), mod4((second if out else first) - i)]
        return copy(at, at, ks_s.at[r, i], ks_r.at[r, i], sib)

    def depth(c):
        return pl.ds(c * 256, 256)

    def w_out(to, c):
        dst = wb.at[k, z, x, depth(c)]
        return copy(wsrc.at[depth(c)], dst, wz_s.at[c, to], wz_r.at[c, z], device(to, x, y, h, k))

    def w_remote(to):
        return (h != to) | (z != h)

    def w_in(j, c):
        from_z = mod4(z + j)
        at = wb.at[k, from_z, x, depth(c)]
        return copy(at, at, wz_s.at[c, 0], wz_r.at[c, from_z], device(z, x, y, from_z, k))

    def w_x(j, i, c, out):
        at = wb.at[k, mod4(z + j), x if out else mod4(x - i), depth(c)]
        return copy(at, at, wx_s.at[c, j, i], wx_r.at[c, j, i], device(h, x + i, y, z, k))

    def w_sib(j, c, out):
        at = wb.at[k if out else other, mod4(z + j), :, depth(c)]
        return copy(at, at, ws_s.at[c, j], ws_r.at[c, j], sib)

    def a_z(i, dk, out):
        core = lax.rem(k + dk, 2)
        dst = ar.at[z, k, y] if out else ar.at[mod4(z - i), core, y]
        return copy(asrc.at[core], dst, az_s.at[i, dk], az_r.at[i, dk], device(h, x, y, z + i, core))

    def a_y(i, dy, out):
        at = ar.at[mod4(z - i), :, y if out else mod4(y - dy)]
        return copy(at, at, ay_s.at[i, dy], ay_r.at[i, dy], device(h, x, y + dy, z, k))

    def o_y(dy, dk, out):
        core = lax.rem(k + dk, 2)
        dst = ob.at[k, y] if out else ob.at[core, mod4(y - dy)]
        return copy(osrc.at[mod4(y + dy), core], dst, o_s.at[dy, dk], o_r.at[dy, dk], device(h, x, y + dy, z, core))

    pairs = [(i, dk) for i in range(4) for dk in range(2) if i or dk]

    def first_out(r):
        for i in (2, 1, 3):
            kv_first(r, i, True).start()

    def second_out(r):
        for i in (1, 3, 2):
            kv_first(r, i, False).wait_recv()
        for i in (2, 1, 3):
            kv_second(r, i, True).start()
        kv_sib(r, 0, True).start()

    def sib_out(r):
        for i in (1, 3, 2):
            kv_second(r, i, False).wait_recv()
            kv_sib(r, i, True).start()

    def attend(hp, line, own_plane):
        keys = kv[0, hp, line, :, 0:ROWS, :].reshape(4 * ROWS, HD)
        values = kv[1, hp, :, pl.ds(line, 1), 0:ROWS, :].reshape(4 * ROWS, HD)
        ids = kv[0, hp, line, :, ROWS:BLK, :].astype(F32)
        ids = jnp.concatenate([ids[j, 0:1, :] for j in range(4)], axis=1)
        scores = lax.dot_general(
            q_ref[...], keys, (((1,), (1,)), ((), ())), preferred_element_type=F32
        )
        own = segq[...]
        allowed = ids == jnp.concatenate([own] * 4, axis=1)
        if own_plane:
            lane = lax.broadcasted_iota(jnp.int32, scores.shape, 1)
            place = lane + (lane >> 7) * (3 * ROWS) + line * ROWS
            token = (lax.broadcasted_iota(jnp.int32, scores.shape, 0) & (ROWS - 1)) + (x * 4 + y) * ROWS
            allowed = allowed & (place <= token)
        scores = jnp.where(allowed, scores, NEG)
        before = top[...]
        now = jnp.maximum(before, jnp.max(scores, axis=1, keepdims=True))
        rate = math.log2(math.e) / math.sqrt(HD)
        keep = jnp.exp2((before - now) * rate)
        weights = jnp.exp2((scores - jnp.concatenate([now] * 4, axis=1)) * rate)
        part = (weights[:, 0:128] + weights[:, 128:256]) + (weights[:, 256:384] + weights[:, 384:512])
        top[...] = now
        den[...] = den[...] * keep + part
        acc[...] = acc[...] * keep + jnp.dot(weights.astype(BF16), values, preferred_element_type=F32)

    def attend_plane(r):
        def line(i, _):
            kv_sib(r, i, False).wait_recv()
            return 0

        lax.fori_loop(0, 4, line, 0)

        def lines(i, _):
            attend(mod4(h - r), mod4(y - i), r == 0)
            return 0

        lax.fori_loop(0, 4, lines, 0)

    def w_start(to, also=True, parts=(0, 1)):
        @pl.when(w_remote(to) & also)
        def _():
            for c in parts:
                w_out(to, c).start()

    def later(r, step):
        @pl.when(r <= h)
        def _():
            step(r)

    def passed_on(r):
        kv_z(r, False).wait_recv()
        first_out(r)

    for i in (2, 1, 3):

        @pl.when(h + i <= 3)
        def _(i=i):
            kv_z(i, True).start()

    first_out(0)

    load(w_in_hbm, w_ref, 2).wait()
    rotated = jnp.dot(w_ref[...], hadamard_signs(), preferred_element_type=F32) * (1.0 / math.sqrt(HD))
    wsrc[...] = rotated.astype(BF16)
    load(q_in, q_raw, 3).wait()
    by_head = q_raw[...].astype(F32)
    for head in range(4):
        q_ref[head * ROWS : (head + 1) * ROWS, :] = by_head[:, head, :].astype(BF16)
    seg_col = jnp.broadcast_to(seg_row, (ROWS, HD)).T
    for i in range(4):
        segq[i * ROWS : (i + 1) * ROWS, :] = seg_col
    top[...] = jnp.full_like(top, NEG)
    den[...] = jnp.zeros_like(den)
    acc[...] = jnp.zeros_like(acc)

    second_out(0)
    for r in (1, 3):
        later(r, passed_on)
    w_start(0)
    w_start(1, h > 0)
    for to in range(1, 4):
        w_start(to, h == 0, (0,))
    later(2, passed_on)

    @pl.when(h == z)
    def _():
        wb[k, z, x] = wsrc[...]

    for r in (1, 3, 2):
        later(r, second_out)
    w_start(2, h > 0)
    w_start(3, h > 0)

    def w_on(j, c):
        if j == 0:

            @pl.when(h != z)
            def _():
                w_in(0, c).wait_recv()
        else:
            w_in(j, c).wait_recv()
        for i in (2, 1, 3):
            w_x(j, i, c, True).start()

    sib_out(0)
    attend_plane(0)
    for r in (1, 3, 2):
        later(r, sib_out)
        later(r, attend_plane)

    out = acc[...] / jnp.sum(den[...], axis=1, keepdims=True)
    for head in range(4):
        for half in range(2):
            start = head * ROWS + half * 64
            asrc[half, :, head * HD : (head + 1) * HD] = out[start : start + 64].astype(BF16)
    for i, dk in pairs:
        a_z(i, dk, True).start()
    ar[z, k, y] = asrc[k]
    for to in range(1, 4):
        w_start(to, h == 0, (1,))
    def a_on(i):
        for dk in range(2):
            if i or dk:
                a_z(i, dk, False).wait_recv()
        for dy in (2, 1, 3):
            a_y(i, dy, True).start()

    a_on(0)
    for j in range(4):
        w_on(j, 0)
    for j, r in enumerate((1, 3, 2)):
        w_on(j, 1)
        a_on(r)
    w_on(3, 1)

    for c in range(2):
        for j in range(4):
            for i in range(1, 4):
                w_x(j, i, c, False).wait_recv()
            w_sib(j, c, True).start()
    for c in range(2):
        for j in range(4):
            w_sib(j, c, False).wait_recv()

    total = None
    for i in (0, 1, 3, 2):
        for dy in (1, 3, 2):
            a_y(i, dy, False).wait_recv()
        from_z = mod4(z - i)
        for core in range(2):
            rows = ar[from_z, core].reshape(4 * 64, 4 * HD)
            columns = jnp.concatenate([wb[core, from_z, j] for j in range(4)], axis=1)
            term = jnp.dot(rows, columns, preferred_element_type=F32)
            total = term if total is None else total + term

    total = total.astype(BF16)
    for row in range(4):
        for core in range(2):
            for b in range(2):
                col = (core * 2 + b) * HD
                osrc[row, core, b] = total[row * 64 : (row + 1) * 64, col : col + HD]
    for dy, dk in pairs:
        o_y(dy, dk, True).start()
    ob[k, y] = osrc[y, k]
    for dy, dk in pairs:
        o_y(dy, dk, False).wait_recv()
    for core in range(2):
        for row in range(4):
            for b in range(2):
                col = (b * 4 + row) * HD
                o_ref[core * 64 : (core + 1) * 64, col : col + HD] = ob[core, row, b]

    def kv_left(r):
        for i in range(1, 4):
            kv_first(r, i, True).wait_send()
            kv_second(r, i, True).wait_send()
        for i in range(4):
            kv_sib(r, i, True).wait_send()

    kv_left(0)
    for r in range(1, 4):
        later(r, kv_left)

        @pl.when(h + r <= 3)
        def _(r=r):
            kv_z(r, True).wait_send()

    for r in range(4):

        @pl.when(w_remote(r))
        def _(r=r):
            for c in range(2):
                w_out(r, c).wait_send()

        for i in range(1, 4):
            a_y(r, i, True).wait_send()
            for c in range(2):
                w_x(r, i, c, True).wait_send()
        for c in range(2):
            w_sib(r, c, True).wait_send()
    for i, dk in pairs:
        a_z(i, dk, True).wait_send()
        o_y(i, dk, True).wait_send()


def body(queries, keys, values, segment_ids, out_weight):
    dma = pltpu.SemaphoreType.DMA
    return pl.pallas_call(
        kernel,
        out_shape=jax.ShapeDtypeStruct((ROWS, 1024), BF16),
        in_specs=[pl.BlockSpec(memory_space=pl.ANY)] * 5,
        out_specs=pl.BlockSpec(memory_space=pltpu.VMEM),
        scratch_shapes=[
            pltpu.VMEM((ROWS, 4, HD), BF16),
            pltpu.VMEM((ROWS, KVH, HD), BF16),
            pltpu.VMEM((1, ROWS), jnp.int32),
            pltpu.VMEM((512, HD), BF16),
            pltpu.VMEM((512, HD), BF16),
            dma((4,)),
            pltpu.VMEM((2, 4, 4, 4, BLK, HD), BF16),
            pltpu.VMEM((512, HD), BF16),
            pltpu.VMEM((2, 4, 4, 512, HD), BF16),
            pltpu.VMEM((2, 64, 512), BF16),
            pltpu.VMEM((4, 2, 4, 64, 512), BF16),
            pltpu.VMEM((4, 2, 2, 64, HD), BF16),
            pltpu.VMEM((2, 4, 2, 64, HD), BF16),
            pltpu.VMEM((512, HD), F32),
            pltpu.VMEM((512, HD), F32),
            pltpu.VMEM((512, HD), F32),
            pltpu.VMEM((512, HD), F32),
        ]
        + [dma((4,))] * 2
        + [dma((4, 4))] * 6
        + [dma((2, 4))] * 2
        + [dma((2, 4, 4))] * 2
        + [dma((2, 4))] * 2
        + [dma((4, 2))] * 2
        + [dma((4, 4))] * 2
        + [dma((4, 2))] * 2,
        compiler_params=pltpu.CompilerParams(
            collective_id=0, has_side_effects=True, vmem_limit_bytes=60 << 20
        ),
        name="attention_projection",
    )(queries, keys, values, segment_ids.reshape(1, ROWS), out_weight)


def solution(mesh):
    in_specs = (
        P("ctx", "tp", None),
        P("ctx", None, None),
        P("ctx", None, None),
        P("ctx"),
        P("tp", "ctx"),
    )
    return jax.shard_map(body, mesh=mesh, in_specs=in_specs, out_specs=P("ctx", "tp"), check_vma=False)
```

```python
import functools
import math

import jax
import jax.numpy as jnp
from jax import lax
from jax.experimental import pallas as pl
from jax.experimental.pallas import tpu as pltpu
from jax.sharding import PartitionSpec as P

HQ = 32
KVH = 4
HD = 128
ROWS = 128
SEG = 16
BLK = ROWS + SEG
NEG = -1e30
MESH = pl.DeviceIdType.MESH
BF16, F32 = jnp.bfloat16, jnp.float32


def mod4(value):
    return lax.rem(value + 8, 4)


def hadamard_signs():
    both = lax.broadcasted_iota(jnp.int32, (HD, HD), 0) & lax.broadcasted_iota(jnp.int32, (HD, HD), 1)
    both = both ^ (both >> 4)
    both = both ^ (both >> 2)
    both = both ^ (both >> 1)
    return (1 - 2 * (both & 1)).astype(F32).astype(BF16)


def kernel(
    q_in, k_in, v_in, seg_in, w_in_hbm, o_ref,
    q_raw, kv_raw, seg_ref, w_ref, q_ref, in_sem,
    kv, wsrc, wb, asrc, ar, osrc, ob, segq, top, den, acc,
    kz_s, kz_r, ka_s, ka_r, kb_s, kb_r, ks_s, ks_r, wz_s, wz_r, wx_s, wx_r, ws_s, ws_r, az_s, az_r, ay_s, ay_r, o_s, o_r,
):
    ctx, tpi = lax.axis_index("ctx"), lax.axis_index("tp")
    h, x, y = lax.div(ctx, 16), lax.rem(lax.div(ctx, 4), 4), lax.rem(ctx, 4)
    z, k = lax.div(tpi, 2), lax.rem(tpi, 2)
    other = 1 - k
    first = x * other + y * k
    second = y * other + x * k

    def device(h_at, x_at, y_at, z_at, core):
        return (mod4(h_at) * 16 + mod4(x_at) * 4 + mod4(y_at), mod4(z_at) * 2 + core)

    def copy(src, dst, send, recv, target):
        return pltpu.make_async_remote_copy(
            src_ref=src, dst_ref=dst, send_sem=send, recv_sem=recv, device_id=target, device_id_type=MESH
        )

    sib = device(h, x, y, z, other)

    def load(src, dst, i):
        return pltpu.make_async_copy(src, dst, in_sem.at[i])

    @pl.when(k == 0)
    def _():
        load(k_in, kv_raw, 0).start()

    @pl.when(k == 1)
    def _():
        load(v_in, kv_raw, 0).start()

    load(seg_in, seg_ref, 1).start()
    load(w_in_hbm, w_ref, 2).start()
    load(q_in, q_raw, 3).start()

    barrier = pltpu.get_barrier_semaphore()

    def greet(target):
        pl.semaphore_signal(barrier, inc=1, device_id=target, device_id_type=MESH)

    greet(sib)
    for i in range(1, 4):
        greet(device(h, x + i, y, z, k))
        greet(device(h, x, y + i, z, k))
        greet(device(h, x, y + i, z, other))
        greet(device(h, x, y, z + i, other))

    def greet_line(d, _):
        greet(device(h + lax.div(d, 4), x, y, z + lax.rem(d, 4), k))
        return 0

    lax.fori_loop(1, 16, greet_line, 0)

    load(k_in, kv_raw, 0).wait()
    by_head = kv_raw[...].astype(F32)
    for head in range(KVH):

        @pl.when(z == head)
        def _(head=head):
            kv[k, h, second, first, 0:ROWS, :] = by_head[:, head, :].astype(BF16)

    load(seg_in, seg_ref, 1).wait()
    seg_row = seg_ref[...].astype(F32)
    kv[k, h, second, first, ROWS:BLK, :] = jnp.broadcast_to(seg_row, (SEG, HD)).astype(BF16)
    pl.semaphore_wait(barrier, 28)

    def kv_z(i, out):
        at = kv.at[k, h if out else mod4(h - i), second, first]
        return copy(at, at, kz_s.at[i], kz_r.at[i], device(h + i, x, y, z, k))

    def kv_first(r, i, out):
        at = kv.at[k, mod4(h - r), second, first if out else mod4(first - i)]
        return copy(at, at, ka_s.at[r, i], ka_r.at[r, i], device(h, x + i * other, y + i * k, z, k))

    def kv_second(r, i, out):
        at = kv.at[k, mod4(h - r), second if out else mod4(second - i)]
        return copy(at, at, kb_s.at[r, i], kb_r.at[r, i], device(h, x + i * k, y + i * other, z, k))

    def kv_sib(r, i, out):
        at = kv.at[k if out else other, mod4(h - r), mod4((second if out else first) - i)]
        return copy(at, at, ks_s.at[r, i], ks_r.at[r, i], sib)

    def depth(c):
        return pl.ds(c * 256, 256)

    def w_out(to, c):
        dst = wb.at[k, z, x, depth(c)]
        return copy(wsrc.at[depth(c)], dst, wz_s.at[c, to], wz_r.at[c, z], device(to, x, y, h, k))

    def w_remote(to):
        return (h != to) | (z != h)

    def w_in(j, c):
        from_z = mod4(z + j)
        at = wb.at[k, from_z, x, depth(c)]
        return copy(at, at, wz_s.at[c, 0], wz_r.at[c, from_z], device(z, x, y, from_z, k))

    def w_x(j, i, c, out):
        at = wb.at[k, mod4(z + j), x if out else mod4(x - i), depth(c)]
        return copy(at, at, wx_s.at[c, j, i], wx_r.at[c, j, i], device(h, x + i, y, z, k))

    def w_sib(j, c, out):
        at = wb.at[k if out else other, mod4(z + j), :, depth(c)]
        return copy(at, at, ws_s.at[c, j], ws_r.at[c, j], sib)

    def a_z(i, dk, out):
        core = lax.rem(k + dk, 2)
        dst = ar.at[z, k, y] if out else ar.at[mod4(z - i), core, y]
        return copy(asrc.at[core], dst, az_s.at[i, dk], az_r.at[i, dk], device(h, x, y, z + i, core))

    def a_y(i, dy, out):
        at = ar.at[mod4(z - i), :, y if out else mod4(y - dy)]
        return copy(at, at, ay_s.at[i, dy], ay_r.at[i, dy], device(h, x, y + dy, z, k))

    def o_y(dy, dk, out):
        core = lax.rem(k + dk, 2)
        dst = ob.at[k, y] if out else ob.at[core, mod4(y - dy)]
        return copy(osrc.at[mod4(y + dy), core], dst, o_s.at[dy, dk], o_r.at[dy, dk], device(h, x, y + dy, z, core))

    pairs = [(i, dk) for i in range(4) for dk in range(2) if i or dk]

    def first_out(r):
        for i in (2, 1, 3):
            kv_first(r, i, True).start()

    def second_out(r):
        for i in (1, 3, 2):
            kv_first(r, i, False).wait_recv()
        for i in (2, 1, 3):
            kv_second(r, i, True).start()
        kv_sib(r, 0, True).start()

    def sib_out(r):
        for i in (1, 3, 2):
            kv_second(r, i, False).wait_recv()
            kv_sib(r, i, True).start()

    def attend(hp, line, own_plane):
        keys = kv[0, hp, line, :, 0:ROWS, :].reshape(4 * ROWS, HD)
        values = kv[1, hp, :, pl.ds(line, 1), 0:ROWS, :].reshape(4 * ROWS, HD)
        ids = kv[0, hp, line, :, ROWS:BLK, :].astype(F32)
        ids = jnp.concatenate([ids[j, 0:1, :] for j in range(4)], axis=1)
        scores = lax.dot_general(
            q_ref[...], keys, (((1,), (1,)), ((), ())), preferred_element_type=F32
        )
        own = segq[...]
        allowed = ids == jnp.concatenate([own] * 4, axis=1)
        if own_plane:
            lane = lax.broadcasted_iota(jnp.int32, scores.shape, 1)
            place = lane + (lane >> 7) * (3 * ROWS) + line * ROWS
            token = (lax.broadcasted_iota(jnp.int32, scores.shape, 0) & (ROWS - 1)) + (x * 4 + y) * ROWS
            allowed = allowed & (place <= token)
        scores = jnp.where(allowed, scores, NEG)
        before = top[...]
        now = jnp.maximum(before, jnp.max(scores, axis=1, keepdims=True))
        rate = math.log2(math.e) / math.sqrt(HD)
        keep = jnp.exp2((before - now) * rate)
        weights = jnp.exp2((scores - jnp.concatenate([now] * 4, axis=1)) * rate)
        part = (weights[:, 0:128] + weights[:, 128:256]) + (weights[:, 256:384] + weights[:, 384:512])
        top[...] = now
        den[...] = den[...] * keep + part
        acc[...] = acc[...] * keep + jnp.dot(weights.astype(BF16), values, preferred_element_type=F32)

    def attend_plane(r):
        def line(i, _):
            kv_sib(r, i, False).wait_recv()
            return 0

        lax.fori_loop(0, 4, line, 0)

        def lines(i, _):
            attend(mod4(h - r), mod4(y - i), r == 0)
            return 0

        lax.fori_loop(0, 4, lines, 0)

    def w_start(to, also=True, parts=(0, 1)):
        @pl.when(w_remote(to) & also)
        def _():
            for c in parts:
                w_out(to, c).start()

    def later(r, step):
        @pl.when(r <= h)
        def _():
            step(r)

    def passed_on(r):
        kv_z(r, False).wait_recv()
        first_out(r)

    for i in (2, 1, 3):

        @pl.when(h + i <= 3)
        def _(i=i):
            kv_z(i, True).start()

    first_out(0)

    load(w_in_hbm, w_ref, 2).wait()
    rotated = jnp.dot(w_ref[...], hadamard_signs(), preferred_element_type=F32) * (1.0 / math.sqrt(HD))
    wsrc[...] = rotated.astype(BF16)
    load(q_in, q_raw, 3).wait()
    by_head = q_raw[...].astype(F32)
    for head in range(4):
        q_ref[head * ROWS : (head + 1) * ROWS, :] = by_head[:, head, :].astype(BF16)
    seg_col = jnp.broadcast_to(seg_row, (ROWS, HD)).T
    for i in range(4):
        segq[i * ROWS : (i + 1) * ROWS, :] = seg_col
    top[...] = jnp.full_like(top, NEG)
    den[...] = jnp.zeros_like(den)
    acc[...] = jnp.zeros_like(acc)

    second_out(0)
    for r in (1, 3):
        later(r, passed_on)
    w_start(0)
    w_start(1, h > 0)
    for to in range(1, 4):
        w_start(to, h == 0, (0,))
    later(2, passed_on)

    @pl.when(h == z)
    def _():
        wb[k, z, x] = wsrc[...]

    for r in (1, 3, 2):
        later(r, second_out)
    w_start(2, h > 0)
    w_start(3, h > 0)

    def w_on(j, c):
        if j == 0:

            @pl.when(h != z)
            def _():
                w_in(0, c).wait_recv()
        else:
            w_in(j, c).wait_recv()
        for i in (2, 1, 3):
            w_x(j, i, c, True).start()

    sib_out(0)
    attend_plane(0)
    for r in (1, 3, 2):
        later(r, sib_out)
        later(r, attend_plane)

    out = acc[...] / jnp.sum(den[...], axis=1, keepdims=True)
    for head in range(4):
        for half in range(2):
            start = head * ROWS + half * 64
            asrc[half, :, head * HD : (head + 1) * HD] = out[start : start + 64].astype(BF16)
    for i, dk in pairs:
        a_z(i, dk, True).start()
    ar[z, k, y] = asrc[k]
    for to in range(1, 4):
        w_start(to, h == 0, (1,))
    def a_on(i):
        for dk in range(2):
            if i or dk:
                a_z(i, dk, False).wait_recv()
        for dy in (1, 3, 2):
            a_y(i, dy, True).start()

    a_on(0)
    for j in range(4):
        w_on(j, 0)
    for j, r in enumerate((1, 3, 2)):
        w_on(j, 1)
        a_on(r)
    w_on(3, 1)

    for c in range(2):
        for j in range(4):
            for i in range(1, 4):
                w_x(j, i, c, False).wait_recv()
            w_sib(j, c, True).start()
    for c in range(2):
        for j in range(4):
            w_sib(j, c, False).wait_recv()

    total = None
    for i in (0, 1, 3, 2):
        for dy in (1, 3, 2):
            a_y(i, dy, False).wait_recv()
        from_z = mod4(z - i)
        for core in range(2):
            rows = ar[from_z, core].reshape(4 * 64, 4 * HD)
            columns = jnp.concatenate([wb[core, from_z, j] for j in range(4)], axis=1)
            term = jnp.dot(rows, columns, preferred_element_type=F32)
            total = term if total is None else total + term

    total = total.astype(BF16)
    for row in range(4):
        for core in range(2):
            for b in range(2):
                col = (core * 2 + b) * HD
                osrc[row, core, b] = total[row * 64 : (row + 1) * 64, col : col + HD]
    for dy, dk in pairs:
        o_y(dy, dk, True).start()
    ob[k, y] = osrc[y, k]
    for dy, dk in pairs:
        o_y(dy, dk, False).wait_recv()
    for core in range(2):
        for row in range(4):
            for b in range(2):
                col = (b * 4 + row) * HD
                o_ref[core * 64 : (core + 1) * 64, col : col + HD] = ob[core, row, b]

    def kv_left(r):
        for i in range(1, 4):
            kv_first(r, i, True).wait_send()
            kv_second(r, i, True).wait_send()
        for i in range(4):
            kv_sib(r, i, True).wait_send()

    kv_left(0)
    for r in range(1, 4):
        later(r, kv_left)

        @pl.when(h + r <= 3)
        def _(r=r):
            kv_z(r, True).wait_send()

    for r in range(4):

        @pl.when(w_remote(r))
        def _(r=r):
            for c in range(2):
                w_out(r, c).wait_send()

        for i in range(1, 4):
            a_y(r, i, True).wait_send()
            for c in range(2):
                w_x(r, i, c, True).wait_send()
        for c in range(2):
            w_sib(r, c, True).wait_send()
    for i, dk in pairs:
        a_z(i, dk, True).wait_send()
        o_y(i, dk, True).wait_send()


def body(queries, keys, values, segment_ids, out_weight):
    dma = pltpu.SemaphoreType.DMA
    return pl.pallas_call(
        kernel,
        out_shape=jax.ShapeDtypeStruct((ROWS, 1024), BF16),
        in_specs=[pl.BlockSpec(memory_space=pl.ANY)] * 5,
        out_specs=pl.BlockSpec(memory_space=pltpu.VMEM),
        scratch_shapes=[
            pltpu.VMEM((ROWS, 4, HD), BF16),
            pltpu.VMEM((ROWS, KVH, HD), BF16),
            pltpu.VMEM((1, ROWS), jnp.int32),
            pltpu.VMEM((512, HD), BF16),
            pltpu.VMEM((512, HD), BF16),
            dma((4,)),
            pltpu.VMEM((2, 4, 4, 4, BLK, HD), BF16),
            pltpu.VMEM((512, HD), BF16),
            pltpu.VMEM((2, 4, 4, 512, HD), BF16),
            pltpu.VMEM((2, 64, 512), BF16),
            pltpu.VMEM((4, 2, 4, 64, 512), BF16),
            pltpu.VMEM((4, 2, 2, 64, HD), BF16),
            pltpu.VMEM((2, 4, 2, 64, HD), BF16),
            pltpu.VMEM((512, HD), F32),
            pltpu.VMEM((512, HD), F32),
            pltpu.VMEM((512, HD), F32),
            pltpu.VMEM((512, HD), F32),
        ]
        + [dma((4,))] * 2
        + [dma((4, 4))] * 6
        + [dma((2, 4))] * 2
        + [dma((2, 4, 4))] * 2
        + [dma((2, 4))] * 2
        + [dma((4, 2))] * 2
        + [dma((4, 4))] * 2
        + [dma((4, 2))] * 2,
        compiler_params=pltpu.CompilerParams(
            collective_id=0, has_side_effects=True, vmem_limit_bytes=60 << 20
        ),
        name="attention_projection",
    )(queries, keys, values, segment_ids.reshape(1, ROWS), out_weight)


def solution(mesh):
    in_specs = (
        P("ctx", "tp", None),
        P("ctx", None, None),
        P("ctx", None, None),
        P("ctx"),
        P("tp", "ctx"),
    )
    return jax.shard_map(body, mesh=mesh, in_specs=in_specs, out_specs=P("ctx", "tp"), check_vma=False)
```
